32 devices in a mesh: groups: 2 (over y), leaf: 8 (over z, x), sub: 2 (over core).
Axes of the slice: x: 2, y: 2, z: 4, core: 2. Of those that a mesh axis runs over, the one named last changes fastest.
Arguments:
- multipoles: bfloat16 [8192, 64], P(('groups', 'leaf', 'sub')), parts along dimension 0, may hold values from -6 to 6
- list_src: int32 [8192, 189], P(('groups', 'leaf', 'sub')), parts along dimension 0, may hold values from 0 to 639, as said below
- list_mask: int32 [8192, 189], P(('groups', 'leaf', 'sub')), parts along dimension 0, may hold values 0 or 1
- send_boxes: int32 [32, 8, 16], P(('groups', 'leaf', 'sub')), parts along dimension 0, may hold values from 0 to 255
- send_count: int32 [32, 8], P(('groups', 'leaf', 'sub')), parts along dimension 0, may hold values from 0 to 16, as said below
- coarse_src: int32 [128, 189], P(('groups', 'leaf', 'sub')), parts along dimension 0, may hold values from 0 to 63
- coarse_mask: int32 [128, 189], P(('groups', 'leaf', 'sub')), parts along dimension 0, may hold values 0 or 1
- m2l_ops: bfloat16 [316, 64, 64], replicated, may hold values from -0.0546875 to 0.0546875
- m2m_ops: float32 [8, 64, 64], replicated, may hold values from -0.25 to 0.25
- l2l_ops: float32 [8, 64, 64], replicated, may hold values from -0.75 to 0.75
Outputs:
- leaf_locals: float32 [8192, 64], P(('groups', 'leaf', 'sub')), parts along dimension 0
The draws below stay inside these ranges and needn't reach their ends.
There are 2 independent parts, one for each index of `groups`. The reference program is written for one: setup_inputs(seed, part) draws one part's arguments, and reference() takes and returns one part's arrays. A program takes and returns all parts, laid end to end along the dimension named above; an argument that names none is the same for every part. Nothing has to cross between parts.
Inputs may be any that keep to these rules, and one draw needn't show every extreme that they name: `list_src`: an entry e at or above 512 names a leaf index (e - 512) // 16 that differs from the target device's own leaf index in exactly one bit, and a slot below that sender's count toward the target's leaf index. `send_count`: nonzero exactly toward the leaf indices that differ from the sender's own leaf index in one bit; each sender has 16 toward at least one of them.
All inputs are finite; a program needn't handle non-finite values. No bound on the sum of `list_mask` or of `coarse_mask` on one device may be relied on, other than what follows from the above.
Results may differ from the reference program's by a relative error of at most 0.0022.
Values may be sent and summed in bfloat16 or wider, within the bound.
A program may use at most 128 MiB of HBM per device.

```python
import jax
import jax.numpy as jnp
import numpy as np
from jax import lax

COEFFS = 64
LIST = 189
VECS = 316
BOX_DEV = 256
CAP = 16
LEVELS = 2
BOXES = 4096
COARSE_BOXES = 64
N_LEAF = 8
N_SUB = 2


def partner_counts(key):
    devices = N_LEAF * N_SUB
    bit_count = N_LEAF.bit_length() - 1
    key = jax.random.fold_in(key, 11)
    draw_a, draw_b = jax.random.split(key)
    amounts = jax.random.randint(draw_a, (devices, bit_count), 1, CAP + 1, dtype=jnp.int32)
    leaf_ids = jnp.arange(devices, dtype=jnp.int32) // N_SUB
    forced = jax.random.randint(draw_b, (devices,), 0, bit_count, dtype=jnp.int32)
    forced = jnp.where(leaf_ids == N_LEAF - 1, 0, forced)
    positions = jnp.arange(bit_count, dtype=jnp.int32)
    amounts = jnp.where(positions[None, :] == forced[:, None], CAP, amounts)
    partners = jnp.bitwise_xor(leaf_ids[:, None], jnp.left_shift(jnp.int32(1), positions)[None, :])
    peer_ids = jnp.arange(N_LEAF, dtype=jnp.int32)
    matches = partners[:, :, None] == peer_ids[None, None, :]
    return jnp.sum(jnp.where(matches, amounts[:, :, None], 0), axis=1).astype(jnp.int32)


def draw_send_count(key, part):
    return partner_counts(key)


def draw_list_src(key, part):
    amounts = partner_counts(key)
    key = jax.random.fold_in(key, 5)
    subkeys = jax.random.split(key, 4)
    bit_count = N_LEAF.bit_length() - 1
    row_count = BOX_DEV * N_LEAF * N_SUB
    chip_size = N_SUB * BOX_DEV
    device_ids = jnp.arange(row_count, dtype=jnp.int32) // BOX_DEV
    leaf_ids = (device_ids // N_SUB)[:, None]
    core_ids = (device_ids % N_SUB)[:, None]
    remote = jax.random.randint(subkeys[0], (row_count, LIST), 0, 4, dtype=jnp.int32) == 0
    nearby = jax.random.randint(subkeys[1], (row_count, LIST), 0, chip_size, dtype=jnp.int32)
    position = jax.random.randint(subkeys[2], (row_count, LIST), 0, bit_count, dtype=jnp.int32)
    partner = jnp.bitwise_xor(leaf_ids, jnp.left_shift(jnp.int32(1), position))
    sender = partner * N_SUB + core_ids
    slot_limit = amounts[sender, jnp.broadcast_to(leaf_ids, sender.shape)]
    slot_pick = jax.random.randint(subkeys[3], (row_count, LIST), 0, 1 << 20, dtype=jnp.int32) % slot_limit
    far_entry = chip_size + partner * CAP + slot_pick
    entries = jnp.where(remote, far_entry, nearby)
    marked = (N_LEAF - 2) * N_SUB * BOX_DEV
    entries = entries.at[marked, 0].set(chip_size + N_LEAF * CAP - 1)
    entries = entries.at[marked, 1].set(0)
    return entries.astype(jnp.int32)


def plant(result, own_key, low, largest):
    index_at = [jax.random.randint(jax.random.fold_in(own_key, axis), (), 0, length) for axis, length in enumerate(result.shape)]
    longest = result.shape.index(max(result.shape))
    beside = index_at[:longest] + [(index_at[longest] + 1) % result.shape[longest]] + index_at[longest + 1:]
    return result.at[tuple(index_at)].set(low).at[tuple(beside)].set(largest)


def block_levels(own_key, extent, pieces, least, top_value):
    gain, own = 1.0, jax.random.fold_in(own_key, 6)
    for axis_at, blocks in pieces:
        heights = jnp.exp(jax.random.uniform(jax.random.fold_in(own, axis_at), (blocks,), jnp.float32, least / len(pieces), top_value / len(pieces)))
        gain = gain * jnp.repeat(heights, extent[axis_at] // blocks).reshape([-1 if axis == axis_at else 1 for axis in range(len(extent))])
    return gain


def centred(own_key, shape, deviation, limit, pieces=(), kind=jnp.bfloat16):
    drawn = jax.random.normal(own_key, shape, jnp.float32) * deviation
    if len(pieces) > 0:
        drawn = block_levels(own_key, shape, pieces, -0.22, 0.18) * drawn
    return jnp.clip(drawn, min=-limit, max=limit).astype(kind)


def setup_inputs(seed: int = 0, part: int = 0) -> dict:
    keys = jax.random.split(jax.random.key(seed), 11)
    own_keys = jax.random.split(jax.random.fold_in(keys[10], part), 11)
    return {
        "multipoles": centred(own_keys[0], (BOXES, COEFFS), 1.0, 6.0, ((0, 16),)),
        "list_src": draw_list_src(jax.random.fold_in(jax.random.fold_in(keys[10], part), 71), part),
        "list_mask": plant((jax.random.randint(own_keys[2], (BOXES, LIST), 0, 4) < 3).astype(jnp.int32), jax.random.fold_in(own_keys[2], 1), 0, 1),
        "send_boxes": plant(jax.random.randint(own_keys[3], (N_LEAF * N_SUB, N_LEAF, CAP), 0, BOX_DEV), jax.random.fold_in(own_keys[3], 1), 0, BOX_DEV - 1).astype(jnp.int32),
        "send_count": draw_send_count(jax.random.fold_in(jax.random.fold_in(keys[10], part), 71), part),
        "coarse_src": plant(jax.random.randint(own_keys[5], (COARSE_BOXES, LIST), 0, COARSE_BOXES), jax.random.fold_in(own_keys[5], 1), 0, COARSE_BOXES - 1).astype(jnp.int32),
        "coarse_mask": plant((jax.random.randint(own_keys[6], (COARSE_BOXES, LIST), 0, 4) < 3).astype(jnp.int32), jax.random.fold_in(own_keys[6], 1), 0, 1),
        "m2l_ops": centred(keys[7], (VECS, COEFFS, COEFFS), (LIST * COEFFS) ** -0.5, 0.0546875),
        "m2m_ops": centred(keys[8], (8, COEFFS, COEFFS), (8 * COEFFS) ** -0.5, 0.25, (), jnp.float32),
        "l2l_ops": centred(keys[9], (8, COEFFS, COEFFS), COEFFS ** -0.5, 0.75, (), jnp.float32),
    }


def offset_tables():
    vector_rank = {}
    counter = 0
    for step_x in range(-3, 4):
        for step_y in range(-3, 4):
            for step_z in range(-3, 4):
                if max(abs(step_x), abs(step_y), abs(step_z)) > 1:
                    vector_rank[(step_x, step_y, step_z)] = counter
                    counter += 1
    vector_table = []
    for octant in range(8):
        shifts = [(octant >> position) & 1 for position in range(3)]
        entries = []
        for step_x in range(-2 - shifts[0], 4 - shifts[0]):
            for step_y in range(-2 - shifts[1], 4 - shifts[1]):
                for step_z in range(-2 - shifts[2], 4 - shifts[2]):
                    if max(abs(step_x), abs(step_y), abs(step_z)) > 1:
                        entries.append(vector_rank[(step_x, step_y, step_z)])
        vector_table.append(entries)
    return np.array(vector_table, dtype=np.int32)


def far_field(table_rows, sources, weights, m2l_ops, coeffs):
    vectors = offset_tables()
    count_targets = sources.shape[0]
    grouped_src = sources.reshape(count_targets // 8, 8, -1)
    grouped_wts = weights.reshape(count_targets // 8, 8, -1)
    results = []
    for octant in range(8):
        picked = jnp.take(table_rows, grouped_src[:, octant], axis=0)
        picked = jnp.where(grouped_wts[:, octant, :, None] > 0, picked, jnp.zeros((), picked.dtype))
        flat_ops = jnp.take(m2l_ops, jnp.asarray(vectors[octant]), axis=0).reshape(-1, coeffs)
        results.append(jnp.dot(picked.reshape(picked.shape[0], -1), flat_ops, preferred_element_type=jnp.float32))
    return jnp.stack(results, axis=1).reshape(count_targets, coeffs)


def upward(children, m2m_ops):
    grouped = children.reshape(-1, 8, children.shape[-1])
    return jnp.einsum("noc,ocd->nd", grouped, m2m_ops, precision=lax.Precision.HIGHEST)


def downward(parents, l2l_ops):
    spread = jnp.einsum("nc,ocd->nod", parents, l2l_ops, precision=lax.Precision.HIGHEST)
    return spread.reshape(-1, parents.shape[-1])


def reference(multipoles, list_src, list_mask, send_boxes, send_count, coarse_src, coarse_mask, m2l_ops, m2m_ops, l2l_ops):
    coeffs = multipoles.shape[1]
    count_dev = N_LEAF * N_SUB
    chip_size = N_SUB * BOX_DEV

    def one_device(device):
        leaf_id = device // N_SUB
        core_id = device % N_SUB
        entries = lax.dynamic_slice_in_dim(list_src, device * BOX_DEV, BOX_DEV, 0)
        validity = lax.dynamic_slice_in_dim(list_mask, device * BOX_DEV, BOX_DEV, 0)
        is_local = entries < chip_size
        remote = jnp.maximum(entries - chip_size, 0)
        peer_leaf = remote // CAP
        slot_id = remote % CAP
        sender = peer_leaf * N_SUB + core_id
        sent_box = send_boxes[sender, leaf_id, slot_id]
        sent_live = slot_id < send_count[sender, leaf_id]
        global_ids = jnp.where(is_local, leaf_id * chip_size + entries, sender * BOX_DEV + sent_box).astype(jnp.int32)
        weights = validity * jnp.where(is_local | sent_live, 1, 0).astype(jnp.int32)
        return far_field(multipoles, global_ids, weights, m2l_ops, coeffs)

    far_leaf = lax.map(one_device, jnp.arange(count_dev, dtype=jnp.int32)).reshape(-1, coeffs)
    current = multipoles.astype(jnp.float32)
    for level_step in range(LEVELS):
        current = upward(current, m2m_ops)
    coarse = current.astype(jnp.bfloat16)
    inherited = far_field(coarse, coarse_src, coarse_mask, m2l_ops, coeffs)
    for level_step in range(LEVELS):
        inherited = downward(inherited, l2l_ops)
    return far_leaf + inherited
```

```python
import jax
import jax.numpy as jnp
import numpy as np
from jax import lax
from jax.experimental import pallas as pl
from jax.experimental.pallas import tpu as pltpu
from jax.sharding import PartitionSpec as P

LEVELS = 2
LANES = 128
STEP = 8


def list_positions(vec_lanes, dead):
    vector_rank = {}
    for step_x in range(-3, 4):
        for step_y in range(-3, 4):
            for step_z in range(-3, 4):
                if max(abs(step_x), abs(step_y), abs(step_z)) > 1:
                    vector_rank[step_x, step_y, step_z] = len(vector_rank)
    table = np.full((8, vec_lanes), dead, np.int32)
    for octant in range(8):
        shifts = [octant >> position & 1 for position in range(3)]
        entry = 0
        for step_x in range(-2 - shifts[0], 4 - shifts[0]):
            for step_y in range(-2 - shifts[1], 4 - shifts[1]):
                for step_z in range(-2 - shifts[2], 4 - shifts[2]):
                    if max(abs(step_x), abs(step_y), abs(step_z)) > 1:
                        table[octant, vector_rank[step_x, step_y, step_z]] = entry
                        entry += 1
    return table


def round_up(value, unit):
    return -(-value // unit) * unit


def gather_lanes(values, index):
    return jnp.take_along_axis(values, index, axis=1, mode="promise_in_bounds")


def spread_lists(rows, positions):
    pieces = []
    for out in range(positions.shape[1] // LANES):
        where = positions[:, out * LANES : (out + 1) * LANES]
        low = where & (LANES - 1)
        high = where >> 7
        value = gather_lanes(rows[:, :LANES], low)
        for seg in range(1, rows.shape[1] // LANES):
            other = gather_lanes(rows[:, seg * LANES : (seg + 1) * LANES], low)
            value = jnp.where(high == seg, other, value)
        pieces.append(value)
    return pieces


def leaf_kernel(idx_ref, pos_ref, table_ref, ops_ref, out_ref, low_ref, high_ref, acc_ref):
    steps, coeffs, _ = ops_ref.shape
    targets = idx_ref.shape[1]
    width = table_ref.shape[1]
    segs = table_ref.shape[0] // coeffs
    rows = jnp.transpose(idx_ref[...])
    where = jnp.concatenate([pos_ref[...]] * (targets // 8), axis=0)
    for out, piece in enumerate(spread_lists(rows, where)):
        block = jnp.transpose(piece)
        low_ref[out * LANES : (out + 1) * LANES, :] = (block % width).astype(jnp.float32)
        high_ref[out * LANES : (out + 1) * LANES, :] = block // width
    acc_ref[...] = jnp.zeros_like(acc_ref)
    ladder = lax.broadcasted_iota(jnp.int32, (width, LANES), 0).astype(jnp.float32)
    ladder = ladder.astype(jnp.bfloat16)
    one = jnp.ones((), jnp.bfloat16)
    nothing = jnp.zeros((), jnp.bfloat16)

    def step(at, carry):
        base = pl.multiple_of(at * STEP, STEP)
        lows = low_ref[pl.ds(base, STEP), :]
        highs = high_ref[pl.ds(base, STEP), :]
        picked = []
        for vec in range(STEP):
            columns = []
            for tile in range(targets // LANES):
                low = lows[vec : vec + 1, tile * LANES : (tile + 1) * LANES]
                low = jnp.broadcast_to(low, (16, LANES)).astype(jnp.bfloat16)
                low = jnp.concatenate([low] * (width // 16), axis=0)
                columns.append(jnp.where(low == ladder, one, nothing))
            chosen = jnp.concatenate(columns, axis=1)
            found = jnp.dot(table_ref[...], chosen, preferred_element_type=jnp.float32)
            high = jnp.broadcast_to(highs[vec : vec + 1, :], (coeffs, targets))
            value = jnp.zeros((coeffs, targets), jnp.float32)
            for seg in range(segs):
                value = jnp.where(high == seg, found[seg * coeffs : (seg + 1) * coeffs], value)
            picked.append(value.astype(jnp.bfloat16))
        acc_ref[...] += jnp.dot(
            ops_ref[at], jnp.concatenate(picked, axis=0), preferred_element_type=jnp.float32
        )
        return carry

    lax.fori_loop(0, steps, step, 0)
    out_ref[...] = acc_ref[...]


def leaf_far(idx, positions, table, ops):
    coeffs = ops.shape[1]
    targets = idx.shape[1]
    vec_lanes = positions.shape[1]
    return pl.pallas_call(
        leaf_kernel,
        out_shape=jax.ShapeDtypeStruct((coeffs, targets), jnp.float32),
        in_specs=[pl.BlockSpec(memory_space=pltpu.VMEM)] * 4,
        out_specs=pl.BlockSpec(memory_space=pltpu.VMEM),
        scratch_shapes=[
            pltpu.VMEM((vec_lanes, targets), jnp.float32),
            pltpu.VMEM((vec_lanes, targets), jnp.int32),
            pltpu.VMEM((coeffs, targets), jnp.float32),
        ],
        compiler_params=pltpu.CompilerParams(vmem_limit_bytes=40 * 1024 * 1024),
        cost_estimate=pl.CostEstimate(
            flops=20_000_000_000, bytes_accessed=4_000_000, transcendentals=0
        ),
        name="leaf_far",
    )(idx, positions, table, ops)


def coarse_kernel(idx_ref, pos_ref, table_ref, ops_ref, out_ref):
    coeffs, _, vecs = ops_ref.shape
    pieces = spread_lists(idx_ref[...], pos_ref[...])
    lows = [piece & (LANES - 1) for piece in pieces]
    highs = [piece >> 7 for piece in pieces]
    segs = table_ref.shape[1] // LANES

    def step(at, total):
        base = pl.multiple_of(at * STEP, STEP)
        block = table_ref[pl.ds(base, STEP), :]
        for coeff in range(STEP):
            columns = []
            for low, high in zip(lows, highs):
                value = jnp.zeros(low.shape, jnp.float32)
                for seg in range(segs):
                    row = block[coeff : coeff + 1, seg * LANES : (seg + 1) * LANES]
                    other = gather_lanes(jnp.broadcast_to(row, low.shape), low)
                    value = jnp.where(high == seg, other, value)
                columns.append(value)
            picked = jnp.concatenate(columns, axis=1)[:, :vecs].astype(jnp.bfloat16)
            total += lax.dot_general(
                picked,
                ops_ref[base + coeff],
                (((1,), (1,)), ((), ())),
                preferred_element_type=jnp.float32,
            )
        return total

    out_ref[...] = lax.fori_loop(
        0, coeffs // STEP, step, jnp.zeros(out_ref.shape, jnp.float32)
    )


def coarse_far(idx, positions, table, ops):
    return pl.pallas_call(
        coarse_kernel,
        out_shape=jax.ShapeDtypeStruct((idx.shape[0], ops.shape[0]), jnp.float32),
        in_specs=[pl.BlockSpec(memory_space=pltpu.VMEM)] * 4,
        out_specs=pl.BlockSpec(memory_space=pltpu.VMEM),
        compiler_params=pltpu.CompilerParams(vmem_limit_bytes=40 * 1024 * 1024),
        cost_estimate=pl.CostEstimate(
            flops=2_000_000_000, bytes_accessed=4_000_000, transcendentals=0
        ),
        name="coarse_far",
    )(idx, positions, table, ops)


def upward(children, m2m_ops):
    grouped = children.reshape(-1, 8, children.shape[-1])
    return jnp.einsum("noc,ocd->nd", grouped, m2m_ops, precision=lax.Precision.HIGHEST)


def downward(parents, l2l_ops):
    spread = jnp.einsum("nc,ocd->nod", parents, l2l_ops, precision=lax.Precision.HIGHEST)
    return spread.reshape(-1, parents.shape[-1])


def per_device(
    multipoles,
    list_src,
    list_mask,
    send_boxes,
    send_count,
    coarse_src,
    coarse_mask,
    m2l_ops,
    m2m_ops,
    l2l_ops,
):
    boxes, coeffs = multipoles.shape
    entries = list_src.shape[1]
    vecs = m2l_ops.shape[0]
    count_leaf = lax.axis_size("leaf")
    count_sub = lax.axis_size("sub")
    capacity = send_boxes.shape[2]
    bits = count_leaf.bit_length() - 1
    me = lax.axis_index("leaf")
    chip = boxes * count_sub
    segs = count_sub + -(-bits * capacity // boxes)
    by_coeff = multipoles.T

    current = multipoles.astype(jnp.float32)
    for level_step in range(LEVELS):
        current = upward(current, m2m_ops)
    coarse_rows = current.astype(jnp.bfloat16)
    all_coarse = lax.all_gather(coarse_rows, ("leaf", "sub"), axis=0, tiled=True)

    chip_part = lax.all_gather(by_coeff, "sub", axis=0, tiled=True)
    peers = jnp.bitwise_xor(me, jnp.left_shift(1, jnp.arange(bits, dtype=jnp.int32)))
    is_peer = peers[:, None] == jnp.arange(count_leaf, dtype=jnp.int32)[None, :]
    wanted = jnp.sum(jnp.where(is_peer[:, :, None], send_boxes[0][None], 0), axis=1)
    limit = jnp.sum(jnp.where(is_peer, send_count[0][None], 0), axis=1)
    live = jnp.arange(capacity, dtype=jnp.int32)[None, :] < limit[:, None]
    wanted = jnp.where(live, wanted, -1).reshape(1, -1)
    chosen = (jnp.arange(boxes, dtype=jnp.int32)[:, None] == wanted).astype(multipoles.dtype)
    outgoing = jnp.dot(by_coeff, chosen, preferred_element_type=multipoles.dtype)
    incoming = []
    for bit in range(bits):
        pairs = [(leaf, leaf ^ (1 << bit)) for leaf in range(count_leaf)]
        part = outgoing[:, bit * capacity : (bit + 1) * capacity]
        incoming.append(lax.ppermute(part, "leaf", pairs))
    far_width = (segs - count_sub) * boxes
    incoming = jnp.concatenate(incoming, axis=1)
    incoming = jnp.pad(incoming, ((0, 0), (0, far_width - bits * capacity)))
    incoming = incoming.reshape(coeffs, -1, boxes).transpose(1, 0, 2).reshape(-1, boxes)
    table = jnp.concatenate([chip_part, incoming], axis=0)

    entry_lanes = round_up(entries + 1, LANES)
    vec_lanes = round_up(vecs, LANES)
    positions = list_positions(vec_lanes, entry_lanes - 1)
    source = list_src.T
    remote = source - chip
    distance = jnp.bitwise_xor(remote // capacity, me)
    which = jnp.zeros_like(distance)
    for bit in range(1, bits):
        which += (distance >= (1 << bit)).astype(jnp.int32)
    row = jnp.where(source < chip, source, chip + which * capacity + remote % capacity)
    row = jnp.where(list_mask.T > 0, row, segs * boxes)
    row = jnp.pad(
        row, ((0, entry_lanes - entries), (0, 0)), constant_values=segs * boxes
    )
    steps = -(-vecs // STEP)
    ops = jnp.pad(m2l_ops, ((0, steps * STEP - vecs), (0, 0), (0, 0)))
    ops = ops.reshape(steps, STEP, coeffs, coeffs).transpose(0, 3, 1, 2)
    ops = ops.reshape(steps, coeffs, STEP * coeffs)
    far_leaf = leaf_far(row, jnp.asarray(positions), table, ops)

    count_coarse = coarse_rows.shape[0]
    height = round_up(count_coarse, 8)
    dead = all_coarse.shape[0]
    coarse_lanes = round_up(dead + 1, LANES)
    coarse_table = jnp.pad(
        all_coarse.T.astype(jnp.float32), ((0, 0), (0, coarse_lanes - dead))
    )
    coarse_row = jnp.where(coarse_mask > 0, coarse_src, dead)
    coarse_row = jnp.pad(
        coarse_row,
        ((0, height - count_coarse), (0, entry_lanes - entries)),
        constant_values=dead,
    )
    first_coarse = lax.axis_index(("leaf", "sub")) * count_coarse
    doubled = jnp.asarray(np.concatenate([positions, positions], axis=0))
    coarse_positions = lax.dynamic_slice_in_dim(doubled, first_coarse % 8, height, 0)
    inherited = coarse_far(
        coarse_row, coarse_positions, coarse_table, m2l_ops.transpose(1, 2, 0)
    )[:count_coarse]
    for level_step in range(LEVELS):
        inherited = downward(inherited, l2l_ops)
    return far_leaf.T + inherited


def solution(mesh):
    placed = (
        P(("groups", "leaf", "sub"), None),
        P(("groups", "leaf", "sub"), None),
        P(("groups", "leaf", "sub"), None),
        P(("groups", "leaf", "sub"), None, None),
        P(("groups", "leaf", "sub"), None),
        P(("groups", "leaf", "sub"), None),
        P(("groups", "leaf", "sub"), None),
        P(),
        P(),
        P(),
    )
    return jax.shard_map(
        per_device,
        mesh=mesh,
        in_specs=placed,
        out_specs=P(("groups", "leaf", "sub"), None),
        check_vma=False,
    )
```

```python
import jax
import jax.numpy as jnp
import numpy as np
from jax import lax
from jax.experimental import pallas as pl
from jax.experimental.pallas import tpu as pltpu
from jax.sharding import PartitionSpec as P

LEVELS = 2
LANES = 128
STEP = 8


def list_positions(vec_lanes, dead):
    vector_rank = {}
    for step_x in range(-3, 4):
        for step_y in range(-3, 4):
            for step_z in range(-3, 4):
                if max(abs(step_x), abs(step_y), abs(step_z)) > 1:
                    vector_rank[step_x, step_y, step_z] = len(vector_rank)
    table = np.full((8, vec_lanes), dead, np.int32)
    for octant in range(8):
        shifts = [octant >> position & 1 for position in range(3)]
        entry = 0
        for step_x in range(-2 - shifts[0], 4 - shifts[0]):
            for step_y in range(-2 - shifts[1], 4 - shifts[1]):
                for step_z in range(-2 - shifts[2], 4 - shifts[2]):
                    if max(abs(step_x), abs(step_y), abs(step_z)) > 1:
                        table[octant, vector_rank[step_x, step_y, step_z]] = entry
                        entry += 1
    return table


def round_up(value, unit):
    return -(-value // unit) * unit


def gather_lanes(values, index):
    return jnp.take_along_axis(values, index, axis=1, mode="promise_in_bounds")


def spread_lists(rows, positions):
    pieces = []
    for out in range(positions.shape[1] // LANES):
        where = positions[:, out * LANES : (out + 1) * LANES]
        low = where & (LANES - 1)
        high = where >> 7
        value = gather_lanes(rows[:, :LANES], low)
        for seg in range(1, rows.shape[1] // LANES):
            other = gather_lanes(rows[:, seg * LANES : (seg + 1) * LANES], low)
            value = jnp.where(high == seg, other, value)
        pieces.append(value)
    return pieces


def exchange_kernel(
    mine_ref, boxes_ref, counts_ref, coarse_ref, table_ref, all_coarse_ref,
    outbox, inbox, chip_sems, box_sems, send_sems, recv_sems,
):
    coeffs, boxes = mine_ref.shape
    count_leaf, capacity = boxes_ref.shape
    bits = inbox.shape[0]
    lanes = outbox.shape[1]
    members = all_coarse_ref.shape[0]
    count_sub = members // count_leaf
    leaf = lax.axis_index("leaf")
    sub = lax.axis_index("sub")
    me = leaf * count_sub + sub

    def place(other):
        return {"leaf": other // count_sub, "sub": other % count_sub}

    barrier = pltpu.get_barrier_semaphore()

    def greet(step, carry):
        pl.semaphore_signal(barrier, inc=1, device_id=place(jnp.bitwise_xor(me, step)))
        return carry

    lax.fori_loop(1, members, greet, 0)

    slots = lax.broadcasted_iota(jnp.int32, (1, capacity), 1)
    leaves = lax.broadcasted_iota(jnp.int32, (1, count_leaf), 1)
    wanted = []
    for bit in range(bits):
        peer = jnp.bitwise_xor(leaf, 1 << bit)
        limit = jnp.sum(
            jnp.where(leaves == peer, counts_ref[...], 0), axis=1, keepdims=True
        )
        wanted.append(jnp.where(slots < limit, boxes_ref[pl.ds(peer, 1), :], -1))
    wanted.append(jnp.full((1, lanes - bits * capacity), -1, jnp.int32))
    wanted = jnp.broadcast_to(jnp.concatenate(wanted, axis=1), (boxes, lanes))
    ladder = lax.broadcasted_iota(jnp.int32, (boxes, lanes), 0)
    chosen = jnp.where(wanted == ladder, 1.0, 0.0).astype(jnp.bfloat16)
    outbox[...] = jnp.dot(
        mine_ref[...], chosen, preferred_element_type=jnp.float32
    ).astype(jnp.bfloat16)

    pl.semaphore_wait(barrier, members - 1)
    own = pl.ds(pl.multiple_of(sub * coeffs, coeffs), coeffs)
    chip_copy = pltpu.make_async_remote_copy(
        src_ref=mine_ref,
        dst_ref=table_ref.at[own],
        send_sem=chip_sems.at[0],
        recv_sem=chip_sems.at[1],
        device_id={"sub": 1 - sub},
    )
    chip_copy.start()
    box_copies = []
    for bit in range(bits):
        copy = pltpu.make_async_remote_copy(
            src_ref=outbox,
            dst_ref=inbox.at[bit],
            send_sem=box_sems.at[0, bit],
            recv_sem=box_sems.at[1, bit],
            device_id={"leaf": jnp.bitwise_xor(leaf, 1 << bit)},
        )
        copy.start()
        box_copies.append(copy)

    def coarse_copy(step):
        return pltpu.make_async_remote_copy(
            src_ref=coarse_ref,
            dst_ref=all_coarse_ref.at[me],
            send_sem=send_sems.at[step],
            recv_sem=recv_sems.at[step],
            device_id=place(jnp.bitwise_xor(me, step)),
        )

    def send(step, carry):
        coarse_copy(step).start()
        return carry

    def finish(step, carry):
        coarse_copy(step).wait()
        return carry

    lax.fori_loop(1, members, send, 0)
    all_coarse_ref[pl.ds(me, 1)] = coarse_ref[...][None]
    table_ref[own, :] = mine_ref[...]
    for copy in box_copies:
        copy.wait()
    column = lax.broadcasted_iota(jnp.int32, (coeffs, lanes), 1) // capacity
    far = jnp.zeros((coeffs, lanes), jnp.float32)
    for bit in range(bits):
        far = jnp.where(column == bit, inbox[bit].astype(jnp.float32), far)
    table_ref[count_sub * coeffs :, :lanes] = far.astype(jnp.bfloat16)
    table_ref[count_sub * coeffs :, lanes:] = jnp.zeros(
        (coeffs, boxes - lanes), jnp.bfloat16
    )
    chip_copy.wait()
    lax.fori_loop(1, members, finish, 0)


def exchange(mine, send_boxes, send_count, coarse, members, bits):
    coeffs, boxes = mine.shape
    lanes = round_up(bits * send_boxes.shape[1], LANES)
    return pl.pallas_call(
        exchange_kernel,
        out_shape=(
            jax.ShapeDtypeStruct((3 * coeffs, boxes), jnp.bfloat16),
            jax.ShapeDtypeStruct((members,) + coarse.shape, jnp.float32),
        ),
        in_specs=[pl.BlockSpec(memory_space=pltpu.VMEM)] * 4,
        out_specs=[pl.BlockSpec(memory_space=pltpu.VMEM)] * 2,
        scratch_shapes=[
            pltpu.VMEM((coeffs, lanes), jnp.bfloat16),
            pltpu.VMEM((bits, coeffs, lanes), jnp.bfloat16),
            pltpu.SemaphoreType.DMA((2,)),
            pltpu.SemaphoreType.DMA((2, bits)),
            pltpu.SemaphoreType.DMA((members,)),
            pltpu.SemaphoreType.DMA((members,)),
        ],
        compiler_params=pltpu.CompilerParams(
            collective_id=0, has_side_effects=True, vmem_limit_bytes=24 * 1024 * 1024
        ),
        name="exchange",
    )(mine, send_boxes, send_count, coarse)


def leaf_kernel(
    idx_ref, pos_ref, table_ref, coarse_idx_ref, coarse_pos_ref, coarse_ref, ops_ref,
    out_ref, coarse_out_ref, low_ref, high_ref, picks_ref, acc_ref, coarse_table_ref,
):
    coeffs, _, vecs = ops_ref.shape
    targets = idx_ref.shape[1]
    width = table_ref.shape[1]
    segs = table_ref.shape[0] // coeffs
    vec_rows = picks_ref.shape[1] // coeffs
    tiles = targets // LANES
    rows = jnp.transpose(idx_ref[...])
    where = jnp.concatenate([pos_ref[...]] * (targets // 8), axis=0)
    for out, piece in enumerate(spread_lists(rows, where)):
        block = jnp.transpose(piece)
        low_ref[out * LANES : (out + 1) * LANES, :] = (block % width).astype(jnp.float32)
        high_ref[out * LANES : (out + 1) * LANES, :] = block // width
    acc_ref[...] = jnp.zeros_like(acc_ref)
    ladder = lax.broadcasted_iota(jnp.int32, (width, LANES), 0).astype(jnp.float32)
    ladder = ladder.astype(jnp.bfloat16)
    one = jnp.ones((), jnp.bfloat16)
    nothing = jnp.zeros((), jnp.bfloat16)

    def pick(at, carry):
        base = pl.multiple_of(at * STEP, STEP)
        lows = low_ref[pl.ds(base, STEP), :]
        highs = high_ref[pl.ds(base, STEP), :]
        for vec in range(STEP):
            columns = []
            for tile in range(tiles):
                low = lows[vec : vec + 1, tile * LANES : (tile + 1) * LANES]
                low = jnp.broadcast_to(low, (16, LANES)).astype(jnp.bfloat16)
                low = jnp.concatenate([low] * (width // 16), axis=0)
                columns.append(jnp.where(low == ladder, one, nothing))
            chosen = jnp.concatenate(columns, axis=1)
            found = jnp.dot(table_ref[...], chosen, preferred_element_type=jnp.float32)
            high = jnp.broadcast_to(highs[vec : vec + 1, :], (coeffs, targets))
            value = jnp.zeros((coeffs, targets), jnp.float32)
            for seg in range(segs):
                value = jnp.where(high == seg, found[seg * coeffs : (seg + 1) * coeffs], value)
            for tile in range(tiles):
                picks_ref[tile, pl.ds(base + vec, coeffs, stride=vec_rows), :] = value[
                    :, tile * LANES : (tile + 1) * LANES
                ]
        return carry

    lax.fori_loop(0, vec_rows // STEP, pick, 0)

    def contract(at, carry):
        total = acc_ref[...]
        for step in range(4):
            coeff = at * 4 + step
            base = pl.multiple_of(coeff * vec_rows, STEP)
            block = jnp.concatenate(
                [picks_ref[tile, pl.ds(base, vec_rows), :] for tile in range(tiles)], axis=1
            )
            total += jnp.dot(
                ops_ref[coeff],
                block.astype(jnp.bfloat16)[:vecs],
                preferred_element_type=jnp.float32,
            )
        acc_ref[...] = total
        return carry

    lax.fori_loop(0, coeffs // 4, contract, 0)
    out_ref[...] = acc_ref[...]

    coarse_segs = coarse_ref.shape[0] // LANES
    for seg in range(coarse_segs):
        coarse_table_ref[:, seg * LANES : (seg + 1) * LANES] = jnp.transpose(
            coarse_ref[seg * LANES : (seg + 1) * LANES, :]
        )
    pieces = spread_lists(coarse_idx_ref[...], coarse_pos_ref[...])
    lows = [piece & (LANES - 1) for piece in pieces]
    highs = [piece >> 7 for piece in pieces]

    def coarse_step(at, total):
        base = pl.multiple_of(at * STEP, STEP)
        block = coarse_table_ref[pl.ds(base, STEP), :]
        for coeff in range(STEP):
            columns = []
            for low, high in zip(lows, highs):
                value = jnp.zeros(low.shape, jnp.float32)
                for seg in range(coarse_segs):
                    row = block[coeff : coeff + 1, seg * LANES : (seg + 1) * LANES]
                    other = gather_lanes(jnp.broadcast_to(row, low.shape), low)
                    value = jnp.where(high == seg, other, value)
                columns.append(value)
            picked = jnp.concatenate(columns, axis=1)[:, :vecs].astype(jnp.bfloat16)
            total += lax.dot_general(
                picked,
                ops_ref[base + coeff],
                (((1,), (1,)), ((), ())),
                preferred_element_type=jnp.float32,
            )
        return total

    coarse_out_ref[...] = lax.fori_loop(
        0, coeffs // STEP, coarse_step, jnp.zeros(coarse_out_ref.shape, jnp.float32)
    )


def leaf_far(idx, positions, table, coarse_idx, coarse_positions, coarse, ops):
    coeffs, _, vecs = ops.shape
    targets = idx.shape[1]
    vec_lanes = positions.shape[1]
    vec_rows = round_up(vecs, 16)
    return pl.pallas_call(
        leaf_kernel,
        out_shape=(
            jax.ShapeDtypeStruct((coeffs, targets), jnp.float32),
            jax.ShapeDtypeStruct((coarse_idx.shape[0], coeffs), jnp.float32),
        ),
        in_specs=[pl.BlockSpec(memory_space=pltpu.VMEM)] * 7,
        out_specs=[pl.BlockSpec(memory_space=pltpu.VMEM)] * 2,
        scratch_shapes=[
            pltpu.VMEM((vec_lanes, targets), jnp.float32),
            pltpu.VMEM((vec_lanes, targets), jnp.int32),
            pltpu.VMEM((targets // LANES, coeffs * vec_rows, LANES), jnp.float32),
            pltpu.VMEM((coeffs, targets), jnp.float32),
            pltpu.VMEM((LANES, coarse.shape[0]), jnp.float32),
        ],
        compiler_params=pltpu.CompilerParams(vmem_limit_bytes=48 * 1024 * 1024),
        cost_estimate=pl.CostEstimate(
            flops=20_000_000_000, bytes_accessed=4_000_000, transcendentals=0
        ),
        name="leaf_far",
    )(idx, positions, table, coarse_idx, coarse_positions, coarse, ops)


def upward(children, m2m_ops):
    grouped = children.reshape(-1, 8, children.shape[-1])
    return jnp.einsum("noc,ocd->nd", grouped, m2m_ops, precision=lax.Precision.HIGHEST)


def downward(parents, l2l_ops):
    spread = jnp.einsum("nc,ocd->nod", parents, l2l_ops, precision=lax.Precision.HIGHEST)
    return spread.reshape(-1, parents.shape[-1])


def per_device(
    multipoles,
    list_src,
    list_mask,
    send_boxes,
    send_count,
    coarse_src,
    coarse_mask,
    m2l_ops,
    m2m_ops,
    l2l_ops,
):
    boxes, coeffs = multipoles.shape
    entries = list_src.shape[1]
    vecs = m2l_ops.shape[0]
    count_leaf = lax.axis_size("leaf")
    count_sub = lax.axis_size("sub")
    capacity = send_boxes.shape[2]
    bits = count_leaf.bit_length() - 1
    me = lax.axis_index("leaf")
    chip = boxes * count_sub
    members = count_leaf * count_sub
    segs = count_sub + 1
    by_coeff = multipoles.T

    current = multipoles.astype(jnp.float32)
    for level_step in range(LEVELS):
        current = upward(current, m2m_ops)
    count_coarse = current.shape[0]
    height = round_up(count_coarse + 1, 8)
    coarse_rows = current.astype(jnp.bfloat16).astype(jnp.float32)
    coarse_rows = jnp.pad(
        coarse_rows, ((0, height - count_coarse), (0, LANES - coeffs))
    )
    table, all_coarse = exchange(
        by_coeff, send_boxes[0], send_count, coarse_rows, members, bits
    )

    entry_lanes = round_up(entries + 1, LANES)
    vec_lanes = round_up(vecs, LANES)
    positions = list_positions(vec_lanes, entry_lanes - 1)
    source = list_src.T
    remote = source - chip
    distance = jnp.bitwise_xor(remote // capacity, me)
    which = jnp.zeros_like(distance)
    for bit in range(1, bits):
        which += (distance >= (1 << bit)).astype(jnp.int32)
    row = jnp.where(source < chip, source, chip + which * capacity + remote % capacity)
    row = jnp.where(list_mask.T > 0, row, segs * boxes)
    row = jnp.pad(
        row, ((0, entry_lanes - entries), (0, 0)), constant_values=segs * boxes
    )

    all_coarse = all_coarse.reshape(members * height, LANES)
    all_coarse = jnp.pad(
        all_coarse, ((0, round_up(members * height, LANES) - members * height), (0, 0))
    )
    coarse_row = coarse_src // count_coarse * height + coarse_src % count_coarse
    coarse_row = jnp.where(coarse_mask > 0, coarse_row, count_coarse)
    coarse_row = jnp.pad(
        coarse_row,
        ((0, height - count_coarse), (0, entry_lanes - entries)),
        constant_values=count_coarse,
    )
    first_coarse = lax.axis_index(("leaf", "sub")) * count_coarse
    doubled = jnp.asarray(np.concatenate([positions, positions], axis=0))
    coarse_positions = lax.dynamic_slice_in_dim(doubled, first_coarse % 8, height, 0)
    far_leaf, inherited = leaf_far(
        row,
        jnp.asarray(positions),
        table,
        coarse_row,
        coarse_positions,
        all_coarse,
        m2l_ops.transpose(1, 2, 0),
    )
    inherited = inherited[:count_coarse]
    for level_step in range(LEVELS):
        inherited = downward(inherited, l2l_ops)
    return far_leaf.T + inherited


def solution(mesh):
    placed = (
        P(("groups", "leaf", "sub"), None),
        P(("groups", "leaf", "sub"), None),
        P(("groups", "leaf", "sub"), None),
        P(("groups", "leaf", "sub"), None, None),
        P(("groups", "leaf", "sub"), None),
        P(("groups", "leaf", "sub"), None),
        P(("groups", "leaf", "sub"), None),
        P(),
        P(),
        P(),
    )
    return jax.shard_map(
        per_device,
        mesh=mesh,
        in_specs=placed,
        out_specs=P(("groups", "leaf", "sub"), None),
        check_vma=False,
    )
```

```python
import jax
import jax.numpy as jnp
import numpy as np
from jax import lax
from jax.experimental import pallas as pl
from jax.experimental.pallas import tpu as pltpu
from jax.sharding import PartitionSpec as P

LEVELS = 2
LANES = 128
STEP = 8


def list_positions(vec_lanes, dead):
    vector_rank = {}
    for step_x in range(-3, 4):
        for step_y in range(-3, 4):
            for step_z in range(-3, 4):
                if max(abs(step_x), abs(step_y), abs(step_z)) > 1:
                    vector_rank[step_x, step_y, step_z] = len(vector_rank)
    table = np.full((8, vec_lanes), dead, np.int32)
    for octant in range(8):
        shifts = [octant >> position & 1 for position in range(3)]
        entry = 0
        for step_x in range(-2 - shifts[0], 4 - shifts[0]):
            for step_y in range(-2 - shifts[1], 4 - shifts[1]):
                for step_z in range(-2 - shifts[2], 4 - shifts[2]):
                    if max(abs(step_x), abs(step_y), abs(step_z)) > 1:
                        table[octant, vector_rank[step_x, step_y, step_z]] = entry
                        entry += 1
    return table


def step_plan():
    vector_rank = {}
    for step_x in range(-3, 4):
        for step_y in range(-3, 4):
            for step_z in range(-3, 4):
                if max(abs(step_x), abs(step_y), abs(step_z)) > 1:
                    vector_rank[step_x, step_y, step_z] = len(vector_rank)
    groups = []
    for axes in ((), (0,), (1,), (2,), (0, 1), (0, 2), (1, 2), (0, 1, 2)):
        steps = []
        spans = [(3,) if axis in axes else range(-2, 3) for axis in range(3)]
        for inner in np.ndindex(*[len(span) for span in spans]):
            vector = [span[place] for span, place in zip(spans, inner)]
            if max(abs(part) for part in vector) < 2:
                continue
            ranks = []
            for choice in range(1 << len(axes)):
                signed = list(vector)
                for place, axis in enumerate(axes):
                    signed[axis] = -3 if choice >> place & 1 else 3
                ranks.append(vector_rank[tuple(signed)])
            steps.append(ranks)
        groups.append((axes, steps))
    return groups


def step_tables(positions, lanes, dead):
    entries = np.full((8, lanes), dead, np.int32)
    ranks = np.zeros((lanes, 8), np.int32)
    at = 0
    for axes, steps in step_plan():
        for step in steps:
            for octant in range(8):
                choice = sum((octant >> axis & 1) << place for place, axis in enumerate(axes))
                entries[octant, at] = positions[octant, step[choice]]
            ranks[at, : len(step)] = step
            at += 1
    return entries, ranks


def round_up(value, unit):
    return -(-value // unit) * unit


def gather_lanes(values, index):
    return jnp.take_along_axis(values, index, axis=1, mode="promise_in_bounds")


def spread_lists(rows, positions):
    pieces = []
    for out in range(positions.shape[1] // LANES):
        where = positions[:, out * LANES : (out + 1) * LANES]
        low = where & (LANES - 1)
        high = where >> 7
        value = gather_lanes(rows[:, :LANES], low)
        for seg in range(1, rows.shape[1] // LANES):
            other = gather_lanes(rows[:, seg * LANES : (seg + 1) * LANES], low)
            value = jnp.where(high == seg, other, value)
        pieces.append(value)
    return pieces


def exchange_kernel(
    mine_ref, boxes_ref, counts_ref, coarse_ref, table_ref, all_coarse_ref,
    outbox, inbox, chip_sems, box_sems, send_sems, recv_sems,
):
    coeffs, boxes = mine_ref.shape
    count_leaf, capacity = boxes_ref.shape
    bits = inbox.shape[0]
    lanes = outbox.shape[1]
    members = all_coarse_ref.shape[0]
    count_sub = members // count_leaf
    leaf = lax.axis_index("leaf")
    sub = lax.axis_index("sub")
    me = leaf * count_sub + sub

    def place(other):
        return {"leaf": other // count_sub, "sub": other % count_sub}

    barrier = pltpu.get_barrier_semaphore()

    def greet(step, carry):
        pl.semaphore_signal(barrier, inc=1, device_id=place(jnp.bitwise_xor(me, step)))
        return carry

    lax.fori_loop(1, members, greet, 0)

    slots = lax.broadcasted_iota(jnp.int32, (1, capacity), 1)
    leaves = lax.broadcasted_iota(jnp.int32, (1, count_leaf), 1)
    wanted = []
    for bit in range(bits):
        peer = jnp.bitwise_xor(leaf, 1 << bit)
        limit = jnp.sum(
            jnp.where(leaves == peer, counts_ref[...], 0), axis=1, keepdims=True
        )
        wanted.append(jnp.where(slots < limit, boxes_ref[pl.ds(peer, 1), :], -1))
    wanted.append(jnp.full((1, lanes - bits * capacity), -1, jnp.int32))
    wanted = jnp.broadcast_to(jnp.concatenate(wanted, axis=1), (boxes, lanes))
    ladder = lax.broadcasted_iota(jnp.int32, (boxes, lanes), 0)
    chosen = jnp.where(wanted == ladder, 1.0, 0.0).astype(jnp.bfloat16)
    outbox[...] = jnp.dot(
        mine_ref[...], chosen, preferred_element_type=jnp.float32
    ).astype(jnp.bfloat16)

    pl.semaphore_wait(barrier, members - 1)
    own = pl.ds(pl.multiple_of(sub * coeffs, coeffs), coeffs)
    chip_copy = pltpu.make_async_remote_copy(
        src_ref=mine_ref,
        dst_ref=table_ref.at[own],
        send_sem=chip_sems.at[0],
        recv_sem=chip_sems.at[1],
        device_id={"sub": 1 - sub},
    )
    chip_copy.start()
    box_copies = []
    for bit in range(bits):
        copy = pltpu.make_async_remote_copy(
            src_ref=outbox,
            dst_ref=inbox.at[bit],
            send_sem=box_sems.at[0, bit],
            recv_sem=box_sems.at[1, bit],
            device_id={"leaf": jnp.bitwise_xor(leaf, 1 << bit)},
        )
        copy.start()
        box_copies.append(copy)

    def coarse_copy(step):
        return pltpu.make_async_remote_copy(
            src_ref=coarse_ref,
            dst_ref=all_coarse_ref.at[me],
            send_sem=send_sems.at[step],
            recv_sem=recv_sems.at[step],
            device_id=place(jnp.bitwise_xor(me, step)),
        )

    def send(step, carry):
        coarse_copy(step).start()
        return carry

    def finish(step, carry):
        coarse_copy(step).wait()
        return carry

    lax.fori_loop(1, members, send, 0)
    all_coarse_ref[pl.ds(me, 1)] = coarse_ref[...][None]
    table_ref[own, :] = mine_ref[...]
    for copy in box_copies:
        copy.wait()
    column = lax.broadcasted_iota(jnp.int32, (coeffs, lanes), 1) // capacity
    far = jnp.zeros((coeffs, lanes), jnp.float32)
    for bit in range(bits):
        far = jnp.where(column == bit, inbox[bit].astype(jnp.float32), far)
    table_ref[count_sub * coeffs :, :lanes] = far.astype(jnp.bfloat16)
    table_ref[count_sub * coeffs :, lanes:] = jnp.zeros(
        (coeffs, boxes - lanes), jnp.bfloat16
    )
    chip_copy.wait()
    lax.fori_loop(1, members, finish, 0)


def exchange(mine, send_boxes, send_count, coarse, members, bits):
    coeffs, boxes = mine.shape
    lanes = round_up(bits * send_boxes.shape[1], LANES)
    return pl.pallas_call(
        exchange_kernel,
        out_shape=(
            jax.ShapeDtypeStruct((3 * coeffs, boxes), jnp.bfloat16),
            jax.ShapeDtypeStruct((members,) + coarse.shape, jnp.float32),
        ),
        in_specs=[pl.BlockSpec(memory_space=pltpu.VMEM)] * 4,
        out_specs=[pl.BlockSpec(memory_space=pltpu.VMEM)] * 2,
        scratch_shapes=[
            pltpu.VMEM((coeffs, lanes), jnp.bfloat16),
            pltpu.VMEM((bits, coeffs, lanes), jnp.bfloat16),
            pltpu.SemaphoreType.DMA((2,)),
            pltpu.SemaphoreType.DMA((2, bits)),
            pltpu.SemaphoreType.DMA((members,)),
            pltpu.SemaphoreType.DMA((members,)),
        ],
        compiler_params=pltpu.CompilerParams(
            collective_id=0, has_side_effects=True, vmem_limit_bytes=24 * 1024 * 1024
        ),
        name="exchange",
    )(mine, send_boxes, send_count, coarse)


def leaf_kernel(
    idx_ref, pos_ref, ranks_ref, table_ref, coarse_idx_ref, coarse_pos_ref, coarse_ref, ops_hbm,
    out_ref, coarse_out_ref, low_ref, high_ref, picks_ref, acc_ref, coarse_table_ref, ops_ref,
    ops_sem,
):
    ops_copy = pltpu.make_async_copy(ops_hbm, ops_ref, ops_sem)
    ops_copy.start()
    coeffs, _, vecs = ops_ref.shape
    targets = idx_ref.shape[1]
    width = table_ref.shape[1]
    segs = table_ref.shape[0] // coeffs
    pitch = picks_ref.shape[1] // coeffs
    vec_rows = pitch - 1
    tiles = targets // LANES
    rows = jnp.transpose(idx_ref[...])
    where = jnp.concatenate([pos_ref[...]] * (targets // 8), axis=0)
    for out, piece in enumerate(spread_lists(rows, where)):
        block = jnp.transpose(piece)
        low = (block % width).astype(jnp.float32)
        high = block // width
        for tile in range(tiles):
            lanes = slice(tile * LANES, (tile + 1) * LANES)
            low_ref[tile, out * LANES : (out + 1) * LANES, :] = low[:, lanes]
            high_ref[tile, out * LANES : (out + 1) * LANES, :] = high[:, lanes]
    for row in range(vecs, vec_rows):
        for tile in range(tiles):
            picks_ref[tile, pl.ds(row, coeffs, stride=pitch), :] = jnp.zeros(
                (coeffs, LANES), jnp.float32
            )
    acc_ref[...] = jnp.zeros_like(acc_ref)
    ladder = lax.broadcasted_iota(jnp.int32, (width, LANES), 0).astype(jnp.float32)
    ladder = ladder.astype(jnp.bfloat16)
    one = jnp.ones((), jnp.bfloat16)
    nothing = jnp.zeros((), jnp.bfloat16)
    octants = lax.broadcasted_iota(jnp.int32, (coeffs, LANES), 1) & 7

    def pick(at, axes):
        columns = []
        for tile in range(tiles):
            low = jnp.broadcast_to(low_ref[tile, pl.ds(at, 1), :], (16, LANES))
            low = jnp.concatenate([low.astype(jnp.bfloat16)] * (width // 16), axis=0)
            columns.append(jnp.where(low == ladder, one, nothing))
        chosen = jnp.concatenate(columns, axis=1)
        found = jnp.dot(table_ref[...], chosen, preferred_element_type=jnp.float32)
        bits = jnp.zeros_like(octants)
        for place, axis in enumerate(axes):
            bits += ((octants >> axis) & 1) << place
        for tile in range(tiles):
            high = jnp.broadcast_to(high_ref[tile, pl.ds(at, 1), :], (coeffs, LANES))
            value = jnp.zeros((coeffs, LANES), jnp.float32)
            for seg in range(segs):
                part = found[
                    seg * coeffs : (seg + 1) * coeffs, tile * LANES : (tile + 1) * LANES
                ]
                value = jnp.where(high == seg, part, value)
            for choice in range(1 << len(axes)):
                kept = jnp.where(bits == choice, value, 0.0) if axes else value
                rank = ranks_ref[at, choice]
                picks_ref[tile, pl.ds(rank, coeffs, stride=pitch), :] = kept

    first = 0
    for axes, steps in step_plan():
        unroll = next(n for n in (7, 5, 1) if len(steps) % n == 0)

        def several(turn, carry, axes=axes, first=first, unroll=unroll):
            for inner in range(unroll):
                pick(first + turn * unroll + inner, axes)
            return carry

        lax.fori_loop(0, len(steps) // unroll, several, 0)
        first += len(steps)
    ops_copy.wait()

    def contract(at, carry):
        total = acc_ref[...]
        for step in range(4):
            coeff = at * 4 + step
            block = jnp.concatenate(
                [
                    picks_ref[tile, pl.ds(coeff * pitch, vec_rows), :].astype(jnp.bfloat16)
                    for tile in range(tiles)
                ],
                axis=1,
            )
            total += jnp.dot(
                ops_ref[coeff], block[:vecs], preferred_element_type=jnp.float32
            )
        acc_ref[...] = total
        return carry

    lax.fori_loop(0, coeffs // 4, contract, 0)
    out_ref[...] = acc_ref[...]

    coarse_segs = coarse_ref.shape[0] // LANES
    for seg in range(coarse_segs):
        coarse_table_ref[:, seg * LANES : (seg + 1) * LANES] = jnp.transpose(
            coarse_ref[seg * LANES : (seg + 1) * LANES, :]
        )
    pieces = spread_lists(coarse_idx_ref[...], coarse_pos_ref[...])
    lows = [piece & (LANES - 1) for piece in pieces]
    highs = [piece >> 7 for piece in pieces]

    def coarse_step(at, total):
        base = pl.multiple_of(at * STEP, STEP)
        block = coarse_table_ref[pl.ds(base, STEP), :]
        for coeff in range(STEP):
            columns = []
            for low, high in zip(lows, highs):
                value = jnp.zeros(low.shape, jnp.float32)
                for seg in range(coarse_segs):
                    row = block[coeff : coeff + 1, seg * LANES : (seg + 1) * LANES]
                    other = gather_lanes(jnp.broadcast_to(row, low.shape), low)
                    value = jnp.where(high == seg, other, value)
                columns.append(value)
            picked = jnp.concatenate(columns, axis=1)[:, :vecs].astype(jnp.bfloat16)
            total += lax.dot_general(
                picked,
                ops_ref[base + coeff],
                (((1,), (1,)), ((), ())),
                preferred_element_type=jnp.float32,
            )
        return total

    coarse_out_ref[...] = lax.fori_loop(
        0, coeffs // STEP, coarse_step, jnp.zeros(coarse_out_ref.shape, jnp.float32)
    )


def leaf_far(idx, positions, ranks, table, coarse_idx, coarse_positions, coarse, ops):
    coeffs, _, vecs = ops.shape
    targets = idx.shape[1]
    step_lanes = positions.shape[1]
    vec_rows = round_up(vecs, 16)
    return pl.pallas_call(
        leaf_kernel,
        out_shape=(
            jax.ShapeDtypeStruct((coeffs, targets), jnp.float32),
            jax.ShapeDtypeStruct((coarse_idx.shape[0], coeffs), jnp.float32),
        ),
        in_specs=[
            pl.BlockSpec(memory_space=pltpu.VMEM),
            pl.BlockSpec(memory_space=pltpu.VMEM),
            pl.BlockSpec(memory_space=pltpu.SMEM),
            pl.BlockSpec(memory_space=pltpu.VMEM),
            pl.BlockSpec(memory_space=pltpu.VMEM),
            pl.BlockSpec(memory_space=pltpu.VMEM),
            pl.BlockSpec(memory_space=pltpu.VMEM),
            pl.BlockSpec(memory_space=pl.ANY),
        ],
        out_specs=[pl.BlockSpec(memory_space=pltpu.VMEM)] * 2,
        scratch_shapes=[
            pltpu.VMEM((targets // LANES, step_lanes, LANES), jnp.float32),
            pltpu.VMEM((targets // LANES, step_lanes, LANES), jnp.int32),
            pltpu.VMEM((targets // LANES, coeffs * (vec_rows + 1), LANES), jnp.float32),
            pltpu.VMEM((coeffs, targets), jnp.float32),
            pltpu.VMEM((LANES, coarse.shape[0]), jnp.float32),
            pltpu.VMEM(ops.shape, ops.dtype),
            pltpu.SemaphoreType.DMA,
        ],
        compiler_params=pltpu.CompilerParams(vmem_limit_bytes=48 * 1024 * 1024),
        cost_estimate=pl.CostEstimate(
            flops=20_000_000_000, bytes_accessed=4_000_000, transcendentals=0
        ),
        name="leaf_far",
    )(idx, positions, ranks, table, coarse_idx, coarse_positions, coarse, ops)


def upward(children, m2m_ops):
    grouped = children.reshape(-1, 8, children.shape[-1])
    return jnp.einsum("noc,ocd->nd", grouped, m2m_ops, precision=lax.Precision.HIGHEST)


def downward(parents, l2l_ops):
    spread = jnp.einsum("nc,ocd->nod", parents, l2l_ops, precision=lax.Precision.HIGHEST)
    return spread.reshape(-1, parents.shape[-1])


def per_device(
    multipoles,
    list_src,
    list_mask,
    send_boxes,
    send_count,
    coarse_src,
    coarse_mask,
    m2l_ops,
    m2m_ops,
    l2l_ops,
):
    boxes, coeffs = multipoles.shape
    entries = list_src.shape[1]
    vecs = m2l_ops.shape[0]
    count_leaf = lax.axis_size("leaf")
    count_sub = lax.axis_size("sub")
    capacity = send_boxes.shape[2]
    bits = count_leaf.bit_length() - 1
    me = lax.axis_index("leaf")
    chip = boxes * count_sub
    members = count_leaf * count_sub
    segs = count_sub + 1
    by_coeff = multipoles.T

    current = multipoles.astype(jnp.float32)
    for level_step in range(LEVELS):
        current = upward(current, m2m_ops)
    count_coarse = current.shape[0]
    height = round_up(count_coarse + 1, 8)
    coarse_rows = current.astype(jnp.bfloat16).astype(jnp.float32)
    coarse_rows = jnp.pad(
        coarse_rows, ((0, height - count_coarse), (0, LANES - coeffs))
    )
    table, all_coarse = exchange(
        by_coeff, send_boxes[0], send_count, coarse_rows, members, bits
    )

    entry_lanes = round_up(entries + 1, LANES)
    vec_lanes = round_up(vecs, LANES)
    positions = list_positions(vec_lanes, entry_lanes - 1)
    step_entries, ranks = step_tables(positions, entry_lanes, entry_lanes - 1)
    source = list_src.T
    remote = source - chip
    distance = jnp.bitwise_xor(remote // capacity, me)
    which = jnp.zeros_like(distance)
    for bit in range(1, bits):
        which += (distance >= (1 << bit)).astype(jnp.int32)
    row = jnp.where(source < chip, source, chip + which * capacity + remote % capacity)
    row = jnp.where(list_mask.T > 0, row, segs * boxes)
    row = jnp.pad(
        row, ((0, entry_lanes - entries), (0, 0)), constant_values=segs * boxes
    )

    all_coarse = all_coarse.reshape(members * height, LANES)
    all_coarse = jnp.pad(
        all_coarse, ((0, round_up(members * height, LANES) - members * height), (0, 0))
    )
    coarse_row = coarse_src // count_coarse * height + coarse_src % count_coarse
    coarse_row = jnp.where(coarse_mask > 0, coarse_row, count_coarse)
    coarse_row = jnp.pad(
        coarse_row,
        ((0, height - count_coarse), (0, entry_lanes - entries)),
        constant_values=count_coarse,
    )
    first_coarse = lax.axis_index(("leaf", "sub")) * count_coarse
    doubled = jnp.asarray(np.concatenate([positions, positions], axis=0))
    coarse_positions = lax.dynamic_slice_in_dim(doubled, first_coarse % 8, height, 0)
    far_leaf, inherited = leaf_far(
        row,
        jnp.asarray(step_entries),
        jnp.asarray(ranks),
        table,
        coarse_row,
        coarse_positions,
        all_coarse,
        m2l_ops.transpose(1, 2, 0),
    )
    inherited = inherited[:count_coarse]
    for level_step in range(LEVELS):
        inherited = downward(inherited, l2l_ops)
    return far_leaf.T + inherited


def solution(mesh):
    placed = (
        P(("groups", "leaf", "sub"), None),
        P(("groups", "leaf", "sub"), None),
        P(("groups", "leaf", "sub"), None),
        P(("groups", "leaf", "sub"), None, None),
        P(("groups", "leaf", "sub"), None),
        P(("groups", "leaf", "sub"), None),
        P(("groups", "leaf", "sub"), None),
        P(),
        P(),
        P(),
    )
    return jax.shard_map(
        per_device,
        mesh=mesh,
        in_specs=placed,
        out_specs=P(("groups", "leaf", "sub"), None),
        check_vma=False,
    )
```

```python
import jax
import jax.numpy as jnp
import numpy as np
from jax import lax
from jax.experimental import pallas as pl
from jax.experimental.pallas import tpu as pltpu
from jax.sharding import PartitionSpec as P

LEVELS = 2
LANES = 128
STEP = 8


def list_positions(vec_lanes, dead):
    vector_rank = {}
    for step_x in range(-3, 4):
        for step_y in range(-3, 4):
            for step_z in range(-3, 4):
                if max(abs(step_x), abs(step_y), abs(step_z)) > 1:
                    vector_rank[step_x, step_y, step_z] = len(vector_rank)
    table = np.full((8, vec_lanes), dead, np.int32)
    for octant in range(8):
        shifts = [octant >> position & 1 for position in range(3)]
        entry = 0
        for step_x in range(-2 - shifts[0], 4 - shifts[0]):
            for step_y in range(-2 - shifts[1], 4 - shifts[1]):
                for step_z in range(-2 - shifts[2], 4 - shifts[2]):
                    if max(abs(step_x), abs(step_y), abs(step_z)) > 1:
                        table[octant, vector_rank[step_x, step_y, step_z]] = entry
                        entry += 1
    return table


def step_plan():
    vector_rank = {}
    for step_x in range(-3, 4):
        for step_y in range(-3, 4):
            for step_z in range(-3, 4):
                if max(abs(step_x), abs(step_y), abs(step_z)) > 1:
                    vector_rank[step_x, step_y, step_z] = len(vector_rank)
    groups = []
    for axes in ((), (0,), (1,), (2,), (0, 1), (0, 2), (1, 2), (0, 1, 2)):
        steps = []
        spans = [(3,) if axis in axes else range(-2, 3) for axis in range(3)]
        for inner in np.ndindex(*[len(span) for span in spans]):
            vector = [span[place] for span, place in zip(spans, inner)]
            if max(abs(part) for part in vector) < 2:
                continue
            ranks = []
            for choice in range(1 << len(axes)):
                signed = list(vector)
                for place, axis in enumerate(axes):
                    signed[axis] = -3 if choice >> place & 1 else 3
                ranks.append(vector_rank[tuple(signed)])
            steps.append(ranks)
        groups.append((axes, steps))
    return groups


def step_tables(positions, lanes, dead):
    entries = np.full((8, lanes), dead, np.int32)
    ranks = np.zeros((lanes, 8), np.int32)
    at = 0
    for axes, steps in step_plan():
        for step in steps:
            for octant in range(8):
                choice = sum((octant >> axis & 1) << place for place, axis in enumerate(axes))
                entries[octant, at] = positions[octant, step[choice]]
            ranks[at, : len(step)] = step
            at += 1
    return entries, ranks


def round_up(value, unit):
    return -(-value // unit) * unit


def gather_lanes(values, index):
    return jnp.take_along_axis(values, index, axis=1, mode="promise_in_bounds")


def spread_lists(rows, positions):
    pieces = []
    for out in range(positions.shape[1] // LANES):
        where = positions[:, out * LANES : (out + 1) * LANES]
        low = where & (LANES - 1)
        high = where >> 7
        value = gather_lanes(rows[:, :LANES], low)
        for seg in range(1, rows.shape[1] // LANES):
            other = gather_lanes(rows[:, seg * LANES : (seg + 1) * LANES], low)
            value = jnp.where(high == seg, other, value)
        pieces.append(value)
    return pieces


def exchange_kernel(
    mine_ref, boxes_ref, counts_ref, coarse_ref, table_ref, all_coarse_ref,
    outbox, inbox, chip_sems, box_sems, send_sems, recv_sems,
):
    coeffs, boxes = mine_ref.shape
    count_leaf, capacity = boxes_ref.shape
    bits = inbox.shape[0]
    lanes = outbox.shape[1]
    members = all_coarse_ref.shape[0]
    count_sub = members // count_leaf
    leaf = lax.axis_index("leaf")
    sub = lax.axis_index("sub")
    me = leaf * count_sub + sub

    def place(other):
        return {"leaf": other // count_sub, "sub": other % count_sub}

    barrier = pltpu.get_barrier_semaphore()

    def greet(step, carry):
        pl.semaphore_signal(barrier, inc=1, device_id=place(jnp.bitwise_xor(me, step)))
        return carry

    lax.fori_loop(1, members, greet, 0)

    slots = lax.broadcasted_iota(jnp.int32, (1, capacity), 1)
    leaves = lax.broadcasted_iota(jnp.int32, (1, count_leaf), 1)
    wanted = []
    for bit in range(bits):
        peer = jnp.bitwise_xor(leaf, 1 << bit)
        limit = jnp.sum(
            jnp.where(leaves == peer, counts_ref[...], 0), axis=1, keepdims=True
        )
        wanted.append(jnp.where(slots < limit, boxes_ref[pl.ds(peer, 1), :], -1))
    wanted.append(jnp.full((1, lanes - bits * capacity), -1, jnp.int32))
    wanted = jnp.broadcast_to(jnp.concatenate(wanted, axis=1), (boxes, lanes))
    ladder = lax.broadcasted_iota(jnp.int32, (boxes, lanes), 0)
    chosen = jnp.where(wanted == ladder, 1.0, 0.0).astype(jnp.bfloat16)
    outbox[...] = jnp.dot(
        mine_ref[...], chosen, preferred_element_type=jnp.float32
    ).astype(jnp.bfloat16)

    pl.semaphore_wait(barrier, members - 1)
    own = pl.ds(pl.multiple_of(sub * coeffs, coeffs), coeffs)
    chip_copy = pltpu.make_async_remote_copy(
        src_ref=mine_ref,
        dst_ref=table_ref.at[own],
        send_sem=chip_sems.at[0],
        recv_sem=chip_sems.at[1],
        device_id={"sub": 1 - sub},
    )
    chip_copy.start()
    box_copies = []
    for bit in range(bits):
        copy = pltpu.make_async_remote_copy(
            src_ref=outbox,
            dst_ref=inbox.at[bit],
            send_sem=box_sems.at[0, bit],
            recv_sem=box_sems.at[1, bit],
            device_id={"leaf": jnp.bitwise_xor(leaf, 1 << bit)},
        )
        copy.start()
        box_copies.append(copy)

    def coarse_copy(step):
        return pltpu.make_async_remote_copy(
            src_ref=coarse_ref,
            dst_ref=all_coarse_ref.at[me],
            send_sem=send_sems.at[step],
            recv_sem=recv_sems.at[step],
            device_id=place(jnp.bitwise_xor(me, step)),
        )

    def send(step, carry):
        coarse_copy(step).start()
        return carry

    def finish(step, carry):
        coarse_copy(step).wait()
        return carry

    lax.fori_loop(1, members, send, 0)
    all_coarse_ref[pl.ds(me, 1)] = coarse_ref[...][None]
    table_ref[own, :] = mine_ref[...]
    for copy in box_copies:
        copy.wait()
    column = lax.broadcasted_iota(jnp.int32, (coeffs, lanes), 1) // capacity
    far = jnp.zeros((coeffs, lanes), jnp.float32)
    for bit in range(bits):
        far = jnp.where(column == bit, inbox[bit].astype(jnp.float32), far)
    table_ref[count_sub * coeffs :, :lanes] = far.astype(jnp.bfloat16)
    table_ref[count_sub * coeffs :, lanes:] = jnp.zeros(
        (coeffs, boxes - lanes), jnp.bfloat16
    )
    chip_copy.wait()
    lax.fori_loop(1, members, finish, 0)


def exchange(mine, send_boxes, send_count, coarse, members, bits):
    coeffs, boxes = mine.shape
    lanes = round_up(bits * send_boxes.shape[1], LANES)
    return pl.pallas_call(
        exchange_kernel,
        out_shape=(
            jax.ShapeDtypeStruct((3 * coeffs, boxes), jnp.bfloat16),
            jax.ShapeDtypeStruct((members,) + coarse.shape, jnp.float32),
        ),
        in_specs=[pl.BlockSpec(memory_space=pltpu.VMEM)] * 4,
        out_specs=[pl.BlockSpec(memory_space=pltpu.VMEM)] * 2,
        scratch_shapes=[
            pltpu.VMEM((coeffs, lanes), jnp.bfloat16),
            pltpu.VMEM((bits, coeffs, lanes), jnp.bfloat16),
            pltpu.SemaphoreType.DMA((2,)),
            pltpu.SemaphoreType.DMA((2, bits)),
            pltpu.SemaphoreType.DMA((members,)),
            pltpu.SemaphoreType.DMA((members,)),
        ],
        compiler_params=pltpu.CompilerParams(
            collective_id=0, has_side_effects=True, vmem_limit_bytes=24 * 1024 * 1024
        ),
        name="exchange",
    )(mine, send_boxes, send_count, coarse)


def leaf_kernel(
    idx_ref, pos_ref, ranks_ref, table_ref, coarse_idx_ref, coarse_pos_ref, coarse_ref, ops_hbm,
    out_ref, coarse_out_ref, low_ref, high_ref, picks_ref, acc_ref, coarse_table_ref, ops_ref,
    ops_sem,
):
    ops_copy = pltpu.make_async_copy(ops_hbm, ops_ref, ops_sem)
    ops_copy.start()
    coeffs, _, vecs = ops_ref.shape
    targets = idx_ref.shape[1]
    width = table_ref.shape[1]
    segs = table_ref.shape[0] // coeffs
    pitch = picks_ref.shape[1] // coeffs
    vec_rows = pitch - 1
    tiles = targets // LANES
    rows = jnp.transpose(idx_ref[...])
    where = jnp.concatenate([pos_ref[...]] * (targets // 8), axis=0)
    for out, piece in enumerate(spread_lists(rows, where)):
        block = jnp.transpose(piece)
        low = (block % width).astype(jnp.float32)
        high = block // width
        for tile in range(tiles):
            lanes = slice(tile * LANES, (tile + 1) * LANES)
            low_ref[tile, out * LANES : (out + 1) * LANES, :] = low[:, lanes]
            high_ref[tile, out * LANES : (out + 1) * LANES, :] = high[:, lanes]
    for row in range(vecs, vec_rows):
        for tile in range(tiles):
            picks_ref[tile, pl.ds(row, coeffs, stride=pitch), :] = jnp.zeros(
                (coeffs, LANES), jnp.float32
            )
    acc_ref[...] = jnp.zeros_like(acc_ref)
    ladder = lax.broadcasted_iota(jnp.int32, (width, LANES), 0).astype(jnp.float32)
    ladder = ladder.astype(jnp.bfloat16)
    one = jnp.ones((), jnp.bfloat16)
    nothing = jnp.zeros((), jnp.bfloat16)
    octants = lax.broadcasted_iota(jnp.int32, (coeffs, LANES), 1) & 7

    def pick(at, axes):
        columns = []
        for tile in range(tiles):
            low = jnp.broadcast_to(low_ref[tile, pl.ds(at, 1), :], (16, LANES))
            low = jnp.concatenate([low.astype(jnp.bfloat16)] * (width // 16), axis=0)
            columns.append(jnp.where(low == ladder, one, nothing))
        chosen = jnp.concatenate(columns, axis=1)
        found = jnp.dot(table_ref[...], chosen, preferred_element_type=jnp.float32)
        bits = jnp.zeros_like(octants)
        for place, axis in enumerate(axes):
            bits += ((octants >> axis) & 1) << place
        for tile in range(tiles):
            high = jnp.broadcast_to(high_ref[tile, pl.ds(at, 1), :], (coeffs, LANES))
            value = jnp.zeros((coeffs, LANES), jnp.float32)
            for seg in range(segs):
                part = found[
                    seg * coeffs : (seg + 1) * coeffs, tile * LANES : (tile + 1) * LANES
                ]
                value = jnp.where(high == seg, part, value)
            for choice in range(1 << len(axes)):
                kept = jnp.where(bits == choice, value, 0.0) if axes else value
                rank = ranks_ref[at, choice]
                picks_ref[tile, pl.ds(rank, coeffs, stride=pitch), :] = kept

    first = 0
    for axes, steps in step_plan():
        unroll = next(n for n in (7, 5, 1) if len(steps) % n == 0)

        def several(turn, carry, axes=axes, first=first, unroll=unroll):
            for inner in range(unroll):
                pick(first + turn * unroll + inner, axes)
            return carry

        lax.fori_loop(0, len(steps) // unroll, several, 0)
        first += len(steps)
    ops_copy.wait()

    def contract(at, carry):
        total = acc_ref[...]
        for step in range(4):
            coeff = at * 4 + step
            block = jnp.concatenate(
                [
                    picks_ref[tile, pl.ds(coeff * pitch, vec_rows), :].astype(jnp.bfloat16)
                    for tile in range(tiles)
                ],
                axis=1,
            )
            total += jnp.dot(
                ops_ref[coeff], block[:vecs], preferred_element_type=jnp.float32
            )
        acc_ref[...] = total
        return carry

    lax.fori_loop(0, coeffs // 4, contract, 0)
    out_ref[...] = acc_ref[...]

    coarse_segs = coarse_ref.shape[0] // LANES
    for seg in range(coarse_segs):
        coarse_table_ref[:, seg * LANES : (seg + 1) * LANES] = jnp.transpose(
            coarse_ref[seg * LANES : (seg + 1) * LANES, :]
        )
    me = lax.axis_index("leaf") * lax.axis_size("sub") + lax.axis_index("sub")
    pieces = spread_lists(coarse_idx_ref[...], coarse_pos_ref[jnp.bitwise_and(me, 7)])
    lows = [piece & (LANES - 1) for piece in pieces]
    highs = [piece >> 7 for piece in pieces]

    def coarse_step(at, total):
        base = pl.multiple_of(at * STEP, STEP)
        block = coarse_table_ref[pl.ds(base, STEP), :]
        for coeff in range(STEP):
            columns = []
            for low, high in zip(lows, highs):
                value = jnp.zeros(low.shape, jnp.float32)
                for seg in range(coarse_segs):
                    row = block[coeff : coeff + 1, seg * LANES : (seg + 1) * LANES]
                    other = gather_lanes(jnp.broadcast_to(row, low.shape), low)
                    value = jnp.where(high == seg, other, value)
                columns.append(value)
            picked = jnp.concatenate(columns, axis=1)[:, :vecs].astype(jnp.bfloat16)
            total += lax.dot_general(
                picked,
                ops_ref[base + coeff],
                (((1,), (1,)), ((), ())),
                preferred_element_type=jnp.float32,
            )
        return total

    coarse_out_ref[...] = lax.fori_loop(
        0, coeffs // STEP, coarse_step, jnp.zeros(coarse_out_ref.shape, jnp.float32)
    )


def leaf_far(idx, positions, ranks, table, coarse_idx, coarse_positions, coarse, ops):
    coeffs, _, vecs = ops.shape
    targets = idx.shape[1]
    step_lanes = positions.shape[1]
    vec_rows = round_up(vecs, 16)
    return pl.pallas_call(
        leaf_kernel,
        out_shape=(
            jax.ShapeDtypeStruct((coeffs, targets), jnp.float32),
            jax.ShapeDtypeStruct((coarse_idx.shape[0], coeffs), jnp.float32),
        ),
        in_specs=[
            pl.BlockSpec(memory_space=pltpu.VMEM),
            pl.BlockSpec(memory_space=pltpu.VMEM),
            pl.BlockSpec(memory_space=pltpu.SMEM),
            pl.BlockSpec(memory_space=pltpu.VMEM),
            pl.BlockSpec(memory_space=pltpu.VMEM),
            pl.BlockSpec(memory_space=pltpu.VMEM),
            pl.BlockSpec(memory_space=pltpu.VMEM),
            pl.BlockSpec(memory_space=pl.ANY),
        ],
        out_specs=[pl.BlockSpec(memory_space=pltpu.VMEM)] * 2,
        scratch_shapes=[
            pltpu.VMEM((targets // LANES, step_lanes, LANES), jnp.float32),
            pltpu.VMEM((targets // LANES, step_lanes, LANES), jnp.int32),
            pltpu.VMEM((targets // LANES, coeffs * (vec_rows + 1), LANES), jnp.float32),
            pltpu.VMEM((coeffs, targets), jnp.float32),
            pltpu.VMEM((LANES, coarse.shape[0]), jnp.float32),
            pltpu.VMEM(ops.shape, ops.dtype),
            pltpu.SemaphoreType.DMA,
        ],
        compiler_params=pltpu.CompilerParams(vmem_limit_bytes=60 * 1024 * 1024),
        cost_estimate=pl.CostEstimate(
            flops=20_000_000_000, bytes_accessed=4_000_000, transcendentals=0
        ),
        name="leaf_far",
    )(idx, positions, ranks, table, coarse_idx, coarse_positions, coarse, ops)


def upward(children, m2m_ops):
    grouped = children.reshape(-1, 8, children.shape[-1])
    return jnp.einsum("noc,ocd->nd", grouped, m2m_ops, precision=lax.Precision.HIGHEST)


def downward(parents, l2l_ops):
    spread = jnp.einsum("nc,ocd->nod", parents, l2l_ops, precision=lax.Precision.HIGHEST)
    return spread.reshape(-1, parents.shape[-1])


def per_device(
    multipoles,
    list_src,
    list_mask,
    send_boxes,
    send_count,
    coarse_src,
    coarse_mask,
    m2l_ops,
    m2m_ops,
    l2l_ops,
):
    boxes, coeffs = multipoles.shape
    entries = list_src.shape[1]
    vecs = m2l_ops.shape[0]
    count_leaf = lax.axis_size("leaf")
    count_sub = lax.axis_size("sub")
    capacity = send_boxes.shape[2]
    bits = count_leaf.bit_length() - 1
    me = lax.axis_index("leaf")
    chip = boxes * count_sub
    members = count_leaf * count_sub
    segs = count_sub + 1
    by_coeff = multipoles.T

    current = multipoles.astype(jnp.float32)
    for level_step in range(LEVELS):
        current = upward(current, m2m_ops)
    count_coarse = current.shape[0]
    height = round_up(count_coarse + 1, 8)
    coarse_rows = current.astype(jnp.bfloat16).astype(jnp.float32)
    coarse_rows = jnp.pad(
        coarse_rows, ((0, height - count_coarse), (0, LANES - coeffs))
    )
    table, all_coarse = exchange(
        by_coeff, send_boxes[0], send_count, coarse_rows, members, bits
    )

    entry_lanes = round_up(entries + 1, LANES)
    vec_lanes = round_up(vecs, LANES)
    positions = list_positions(vec_lanes, entry_lanes - 1)
    step_entries, ranks = step_tables(positions, entry_lanes, entry_lanes - 1)
    source = list_src.T
    remote = source - chip
    distance = jnp.bitwise_xor(remote // capacity, me)
    which = jnp.zeros_like(distance)
    for bit in range(1, bits):
        which += (distance >= (1 << bit)).astype(jnp.int32)
    row = jnp.where(source < chip, source, chip + which * capacity + remote % capacity)
    row = jnp.where(list_mask.T > 0, row, segs * boxes)
    row = jnp.pad(
        row, ((0, entry_lanes - entries), (0, 0)), constant_values=segs * boxes
    )

    all_coarse = all_coarse.reshape(members * height, LANES)
    all_coarse = jnp.pad(
        all_coarse, ((0, round_up(members * height, LANES) - members * height), (0, 0))
    )
    coarse_row = coarse_src // count_coarse * height + coarse_src % count_coarse
    coarse_row = jnp.where(coarse_mask > 0, coarse_row, count_coarse)
    coarse_row = jnp.pad(
        coarse_row,
        ((0, height - count_coarse), (0, entry_lanes - entries)),
        constant_values=count_coarse,
    )
    coarse_positions = np.stack(
        [np.roll(positions, -(turn * count_coarse), axis=0)[:height] for turn in range(8)]
    )
    far_leaf, inherited = leaf_far(
        row,
        jnp.asarray(step_entries),
        jnp.asarray(ranks),
        table,
        coarse_row,
        jnp.asarray(coarse_positions),
        all_coarse,
        m2l_ops.transpose(1, 2, 0),
    )
    inherited = inherited[:count_coarse]
    for level_step in range(LEVELS):
        inherited = downward(inherited, l2l_ops)
    return far_leaf.T + inherited


def solution(mesh):
    placed = (
        P(("groups", "leaf", "sub"), None),
        P(("groups", "leaf", "sub"), None),
        P(("groups", "leaf", "sub"), None),
        P(("groups", "leaf", "sub"), None, None),
        P(("groups", "leaf", "sub"), None),
        P(("groups", "leaf", "sub"), None),
        P(("groups", "leaf", "sub"), None),
        P(),
        P(),
        P(),
    )
    return jax.shard_map(
        per_device,
        mesh=mesh,
        in_specs=placed,
        out_specs=P(("groups", "leaf", "sub"), None),
        check_vma=False,
    )
```
